512 devices in a mesh: rep: 64 (over y, x, z_hi), row: 8 (over z_lo, core).
Axes of the slice: x: 4, y: 8, z: 8 (z_hi: 2, z_lo: 4; z = z_hi * 4 + z_lo), core: 2. Of those that a mesh axis runs over, the one named last changes fastest.
Arguments:
- features: bfloat16 [64, 1, 48, 48, 2048], P('rep', None, 'row'), may hold values from -6 to 6
- weights: bfloat16 [64, 3, 3, 2048, 256], P('rep', None, None, 'row'), may hold values from -5 to 5
- upstream: bfloat16 [64, 1, 48, 48, 256], P('rep', None, 'row'), may hold values from -6 to 6
- step_index: int32 [1], replicated, may hold values from 0 to 1023
Outputs:
- new_weights: bfloat16 [64, 3, 3, 2048, 256], P('rep', None, None, 'row')
The draws below stay inside these ranges and needn't reach their ends.
All inputs are finite; a program needn't handle non-finite values.
Results may differ from the reference program's by a relative error of at most 0.0027.
Values may be sent and summed in bfloat16 or wider, within the bound.
A program may use at most 64 MiB of HBM per device.

```python
import jax
import jax.numpy as jnp
from jax import lax

CIN = 2048
COUT = 256
R = 6
B = 1
COLS = 48
HOPS = 4
REPS = 64
ROWS = 48


def block_levels(own_key, shape, shards, least, largest):
    def one(dim, blocks):
        steps = jax.random.uniform(jax.random.fold_in(jax.random.fold_in(own_key, 6), dim), (blocks,), jnp.float32, least / len(shards), largest / len(shards))
        return jnp.repeat(jnp.exp(steps), shape[dim] // blocks).reshape((-1,) + (1,) * (len(shape) - dim - 1))

    gain = one(*shards[0])
    for cut in shards[1:]:
        gain = gain * one(*cut)
    return gain


def noise(own_key, extent, width, bound, pieces=(), dtype=jnp.bfloat16):
    entries = jax.random.normal(own_key, extent, jnp.float32) * width
    if len(pieces) > 0:
        entries = block_levels(own_key, extent, pieces, -0.22, 0.18) * entries
    return jnp.clip(entries, min=-bound, max=bound).astype(dtype)


def setup_inputs(seed: int = 0) -> dict:
    seeds = jax.random.split(jax.random.key(seed), 5)
    features = noise(seeds[0], (REPS, B, ROWS, COLS, CIN), 1.0, 6.0, ((0, 64), (2, 8)))
    weights = noise(seeds[1], (REPS, 3, 3, CIN, COUT), 1.0, 5.0, ((0, 64), (3, 8)))
    upstream = noise(seeds[2], (REPS, B, ROWS, COLS, COUT), 1.0, 6.0, ((0, 64), (2, 8)))
    step_index = jax.random.randint(seeds[3], (1,), 0, 1024).astype(jnp.int32)
    return {"features": features, "weights": weights, "upstream": upstream, "step_index": step_index}


def silu_slope(value):
    sig = jax.nn.sigmoid(value)
    return sig * (1.0 + value * (1.0 - sig))

def one_replica(inputs):
    feats, kernel, upstream = inputs
    chans_in = feats.shape[-1]
    chans_out = kernel.shape[-1]
    padded = jnp.pad(feats, ((0, 0), (R, R), (R, R), (0, 0)))
    scale_in = 1.0 / jnp.sqrt(jnp.float32(9 * chans_in))
    scale_grad = 1.0 / jnp.sqrt(jnp.float32(B * ROWS * COLS))
    windows = []
    for p in range(3):
        for q in range(3):
            win = padded[:, p * R:p * R + ROWS, q * R:q * R + COLS, :]
            windows.append(win.reshape(-1, chans_in))
    pre = jnp.zeros((B * ROWS * COLS, chans_out), jnp.float32)
    for tap in range(9):
        pre = pre + jnp.dot(windows[tap], kernel[tap // 3, tap % 3], preferred_element_type=jnp.float32)
    pre = pre * scale_in
    slope = (upstream.reshape(-1, chans_out).astype(jnp.float32) * silu_slope(pre)).astype(jnp.bfloat16)
    grads = []
    for tap in range(9):
        grads.append(jnp.dot(windows[tap].T, slope, preferred_element_type=jnp.float32) * scale_grad)
    grad = jnp.stack(grads).reshape(3, 3, chans_in, chans_out)
    return grad

def reference(features, weights, upstream, step_index):
    grads = lax.map(one_replica, (features, weights, upstream))
    rate = 1.0 / jnp.sqrt(1.0 + step_index[0].astype(jnp.float32) / 1024.0)
    stepped = weights.astype(jnp.float32) - rate * grads
    offset = jnp.left_shift(jnp.int32(1), (step_index[0] % HOPS).astype(jnp.int32))
    peer = jnp.roll(stepped, offset, axis=0)
    return ((stepped + peer) * 0.5).astype(jnp.bfloat16)
```

```python
from functools import partial

import jax
import jax.numpy as jnp
from jax import lax
from jax.experimental import pallas as pl
from jax.experimental.pallas import tpu as pltpu
from jax.sharding import PartitionSpec as P

R = 6
HOPS = 4
MESH = pl.DeviceIdType.MESH
FAR_FIRST = (2, 1, 3)


def silu_slope(value):
    sig = jax.nn.sigmoid(value)
    return sig * (1.0 + value * (1.0 - sig))


def step_kernel(
    off, cols, scale_in,
    f_ref, w_ref, u_ref, rate_ref, out_ref,
    fcat, wv, uv, pair_tx, pair_rx, sum_tx, sum_rx, slopes, stepped, peer_tx, peer_rx,
    load_sem, move_tx, move_rx, pair_txs, pair_rxs, sum_txs, sum_rxs,
    ring_txs, ring_rxs, fwd_txs, fwd_rxs, peer_txs, peer_rxs,
):
    rows, share = uv.shape[0], wv.shape[1]
    count = lax.axis_size("row")
    chips = count // 2
    reps = lax.axis_size("rep")
    me = lax.axis_index("row")
    rep = lax.axis_index("rep")
    z, c = lax.div(me, 2), lax.rem(me, 2)
    other = 1 - c
    mate = 2 * z + other
    ahead = lax.rem(rep + off, reps)
    behind = lax.rem(rep + reps - off, reps)

    def up(d):
        return lax.rem(z + d, chips)

    def down(d):
        return lax.rem(z + chips - d, chips)

    def rows_of(j):
        return pl.ds(pl.multiple_of(j * rows, rows), rows)

    mid = pl.ds(share, share)

    def load(k, src, dst):
        return pltpu.make_async_copy(src, dst, load_sem.at[k])

    def columns_for(t):
        return f_ref.at[:, pl.ds(pl.multiple_of(t * share, share), share)]

    loads = [
        load(0, columns_for(me), fcat.at[rows_of(me + 1), mid]),
        load(1, w_ref, wv),
        load(2, u_ref, uv),
    ]
    for one in loads:
        one.start()

    barrier = pltpu.get_barrier_semaphore()
    for k in range(1, count):
        to = lax.rem(me + k, count)
        pl.semaphore_signal(barrier, inc=1, device_id={"row": to}, device_id_type=MESH)
    for to in (ahead, behind):
        pl.semaphore_signal(barrier, inc=1, device_id={"rep": to}, device_id_type=MESH)
    pl.semaphore_wait(barrier, count + 1)

    def move(dz, dc):
        to = 2 * up(dz) + lax.rem(c + dc, 2)
        k = 2 * dz + dc
        return pltpu.make_async_remote_copy(
            columns_for(to), fcat.at[rows_of(me + 1), mid],
            move_tx.at[k], move_rx.at[k], device_id={"row": to}, device_id_type=MESH,
        )

    def moved(dz, dc):
        src = 2 * down(dz) + lax.rem(c + dc, 2)
        k = 2 * dz + dc
        copy = pltpu.make_async_remote_copy(
            columns_for(src), fcat.at[rows_of(src + 1), mid],
            move_tx.at[k], move_rx.at[k], device_id={"row": src}, device_id_type=MESH,
        )
        return src, copy

    order = [(dz, dc) for dz in FAR_FIRST for dc in (0, 1)] + [(0, 1)]
    for dz, dc in order:
        move(dz, dc).start()

    edge = jnp.zeros((rows, 3 * share), fcat.dtype)
    fcat[pl.ds(0, rows), :] = edge
    fcat[pl.ds((count + 1) * rows, rows), :] = edge

    col = lax.rem(lax.broadcasted_iota(jnp.int32, (rows, share), 0), cols)

    def shift(j):
        at = rows_of(j + 1)
        x = fcat[at, pl.ds(share, share)].astype(jnp.float32)
        left = jnp.where(col < R, 0.0, pltpu.roll(x, R, 0))
        right = jnp.where(col >= cols - R, 0.0, pltpu.roll(x, rows - R, 0))
        fcat[at, pl.ds(0, share)] = left.astype(fcat.dtype)
        fcat[at, pl.ds(2 * share, share)] = right.astype(fcat.dtype)

    loads[0].wait()
    shift(me)
    for dz, dc in [(0, 1)] + order[:-1]:
        src, copy = moved(dz, dc)
        copy.wait_recv()
        shift(src)
    loads[1].wait()
    loads[2].wait()

    def partial_sum(j):
        total = None
        for p in range(3):
            term = jnp.dot(
                fcat[rows_of(j + p), :], wv[pl.ds(p * 3 * share, 3 * share), :],
                preferred_element_type=jnp.float32,
            )
            total = term if total is None else total + term
        return total

    def pair(dz):
        return pltpu.make_async_remote_copy(
            pair_tx.at[dz], pair_rx.at[dz], pair_txs.at[dz], pair_rxs.at[dz],
            device_id={"row": mate}, device_id_type=MESH,
        )

    def give(dz, ring):
        tx, rx = (sum_txs, sum_rxs)
        return pltpu.make_async_remote_copy(
            sum_tx.at[dz - 1], sum_rx.at[dz - 1], tx.at[dz], rx.at[dz],
            device_id={"row": 2 * up(dz) + c}, device_id_type=MESH,
        )

    for dz in FAR_FIRST + (0,):
        pair_tx[dz] = partial_sum(2 * up(dz) + other).astype(pair_tx.dtype)
        pair(dz).start()
    for dz in FAR_FIRST:
        mine = partial_sum(2 * up(dz) + c)
        pair(dz).wait_recv()
        sum_tx[dz - 1] = (mine + pair_rx[dz].astype(jnp.float32)).astype(sum_tx.dtype)
        give(dz, 0).start()
    pre = partial_sum(me)
    pair(0).wait_recv()
    pre = pre + pair_rx[0].astype(jnp.float32)
    for dz in FAR_FIRST:
        give(dz, 0).wait_recv()
        pre = pre + sum_rx[dz - 1].astype(jnp.float32)
    pre = pre * scale_in
    slopes[rows_of(me), :] = (uv[...].astype(jnp.float32) * silu_slope(pre)).astype(slopes.dtype)

    def spread(dz):
        at = slopes.at[rows_of(me)]
        return pltpu.make_async_remote_copy(
            at, at, ring_txs.at[dz], ring_rxs.at[dz],
            device_id={"row": 2 * up(dz) + c}, device_id_type=MESH,
        )

    def arrived(dz):
        src = 2 * down(dz) + c
        at = slopes.at[rows_of(src)]
        return pltpu.make_async_remote_copy(
            at, at, ring_txs.at[dz], ring_rxs.at[dz],
            device_id={"row": src}, device_id_type=MESH,
        )

    def hand(dz, core):
        at = slopes.at[rows_of(2 * down(dz) + core)]
        return pltpu.make_async_remote_copy(
            at, at, fwd_txs.at[dz], fwd_rxs.at[dz],
            device_id={"row": mate}, device_id_type=MESH,
        )

    for dz in FAR_FIRST:
        spread(dz).start()
    hand(0, c).start()
    for dz in FAR_FIRST:
        arrived(dz).wait_recv()
        hand(dz, c).start()
    for dz in (0,) + FAR_FIRST:
        hand(dz, other).wait_recv()

    rate = rate_ref[0]

    def gossip(p):
        return pltpu.make_async_remote_copy(
            peer_tx.at[p], peer_rx.at[p], peer_txs.at[p], peer_rxs.at[p],
            device_id={"rep": ahead}, device_id_type=MESH,
        )

    height = count * rows
    for p in range(3):
        grad = lax.dot_general(
            fcat[pl.ds(p * rows, height), :], slopes[...],
            (((0,), (0,)), ((), ())), preferred_element_type=jnp.float32,
        )
        new = wv[pl.ds(p * 3 * share, 3 * share), :].astype(jnp.float32) - rate * grad
        stepped[p] = new
        peer_tx[p] = new.astype(peer_tx.dtype)
        gossip(p).start()
    for p in range(3):
        gossip(p).wait_recv()
        out_ref[pl.ds(p * 3 * share, 3 * share), :] = (
            (stepped[p] + peer_rx[p].astype(jnp.float32)) * 0.5
        ).astype(out_ref.dtype)

    for dz, dc in order:
        move(dz, dc).wait_send()
    for dz in range(chips):
        pair(dz).wait_send()
        hand(dz, c).wait_send()
    for dz in FAR_FIRST:
        give(dz, 0).wait_send()
        spread(dz).wait_send()
    for p in range(3):
        gossip(p).wait_send()


def run_step(hop, f, w, u, rate, cols, scale_in):
    rows, chans = f.shape
    taps, outs = w.shape
    count = chans // (taps // 9)
    chips = count // 2
    share = taps // 9
    bf, f32 = jnp.bfloat16, jnp.float32
    dma = pltpu.SemaphoreType.DMA
    anywhere = pl.BlockSpec(memory_space=pl.ANY)
    return pl.pallas_call(
        partial(step_kernel, 1 << hop, cols, scale_in),
        out_shape=jax.ShapeDtypeStruct((taps, outs), bf),
        in_specs=[anywhere, anywhere, anywhere, pl.BlockSpec(memory_space=pltpu.SMEM)],
        out_specs=pl.BlockSpec(memory_space=pltpu.VMEM),
        scratch_shapes=[
            pltpu.VMEM(((count + 2) * rows, 3 * share), bf),
            pltpu.VMEM((taps, outs), bf),
            pltpu.VMEM((rows, outs), bf),
            pltpu.VMEM((chips, rows, outs), f32),
            pltpu.VMEM((chips, rows, outs), f32),
            pltpu.VMEM((chips - 1, rows, outs), bf),
            pltpu.VMEM((chips - 1, rows, outs), bf),
            pltpu.VMEM((count * rows, outs), bf),
            pltpu.VMEM((3, 3 * share, outs), f32),
            pltpu.VMEM((3, 3 * share, outs), bf),
            pltpu.VMEM((3, 3 * share, outs), bf),
            dma((3,)),
            dma((count,)), dma((count,)),
            dma((chips,)), dma((chips,)),
            dma((chips,)), dma((chips,)),
            dma((chips,)), dma((chips,)),
            dma((chips,)), dma((chips,)),
            dma((3,)), dma((3,)),
        ],
        compiler_params=pltpu.CompilerParams(
            collective_id=hop, has_side_effects=True, vmem_limit_bytes=48 << 20
        ),
    )(f, w, u, rate)


def per_device(features, weights, upstream, step_index):
    _, batch, rows_dev, cols, chans_in = features.shape
    share, chans_out = weights.shape[3:]
    rows_all = rows_dev * lax.axis_size("row")
    scale_in = 1.0 / (9 * chans_in) ** 0.5
    scale_grad = 1.0 / jnp.sqrt(jnp.float32(batch * rows_all * cols))
    rate = scale_grad / jnp.sqrt(1.0 + step_index.astype(jnp.float32) / 1024.0)
    f = features.reshape(rows_dev * cols, chans_in)
    w = weights.reshape(9 * share, chans_out)
    u = upstream.reshape(rows_dev * cols, chans_out)
    branches = [partial(run_step, hop, cols=cols, scale_in=scale_in) for hop in range(HOPS)]
    out = lax.switch(step_index[0] % HOPS, branches, f, w, u, rate)
    return out.reshape(weights.shape)


def solution(mesh):
    in_specs = (
        P("rep", None, "row", None, None),
        P("rep", None, None, "row", None),
        P("rep", None, "row", None, None),
        P(),
    )
    out_specs = P("rep", None, None, "row", None)
    return jax.shard_map(
        per_device, mesh=mesh, in_specs=in_specs, out_specs=out_specs, check_vma=False
    )
```

```python
from functools import partial

import jax
import jax.numpy as jnp
from jax import lax
from jax.experimental import pallas as pl
from jax.experimental.pallas import tpu as pltpu
from jax.sharding import PartitionSpec as P

R = 6
HOPS = 4
MESH = pl.DeviceIdType.MESH
FAR_FIRST = (2, 1, 3)
GROUPS = 2


def silu_slope(value):
    sig = jax.nn.sigmoid(value)
    return sig * (1.0 + value * (1.0 - sig))


def step_kernel(
    off, early, hold, cols, scale_in,
    f_ref, w_ref, u_ref, rate_ref, out_ref,
    fcat, wv, uv, acc, pair_rx, sum_tx, sum_rx, slopes, turned, stepped,
    load_sem, move_tx, move_rx, pair_txs, pair_rxs, sum_txs, sum_rxs,
    ring_txs, ring_rxs, fwd_txs, fwd_rxs, *extra,
):
    if early:
        (peer_f, peer_w, peer_s, peer_turned, weight_sems, feat_txs, feat_rxs,
         slope_txs, slope_rxs, share_txs, share_rxs) = extra
    else:
        peer_tx, peer_rx, peer_txs, peer_rxs = extra
    rows, share = uv.shape[0], fcat.shape[1] // 3
    wide = uv.shape[1] // GROUPS
    count = lax.axis_size("row")
    chips = count // 2
    reps = lax.axis_size("rep")
    me = lax.axis_index("row")
    rep = lax.axis_index("rep")
    z, c = lax.div(me, 2), lax.rem(me, 2)
    other = 1 - c
    mate = 2 * z + other
    ahead = lax.rem(rep + off, reps)
    behind = lax.rem(rep + reps - off, reps)
    f32 = jnp.float32

    def up(d):
        return lax.rem(z + d, chips)

    def down(d):
        return lax.rem(z + chips - d, chips)

    def rows_of(j):
        return pl.ds(pl.multiple_of(j * rows, rows), rows)

    def signal(sem, **to):
        pl.semaphore_signal(sem, inc=1, device_id=to, device_id_type=MESH)

    mid = pl.ds(share, share)

    def load(k, src, dst):
        return pltpu.make_async_copy(src, dst, load_sem.at[k])

    def columns_for(t):
        return f_ref.at[:, pl.ds(pl.multiple_of(t * share, share), share)]

    loads = [
        load(0, columns_for(me), fcat.at[rows_of(me + 1), mid]),
        load(1, w_ref, wv),
        load(2, u_ref, uv),
    ]
    for one in loads:
        one.start()

    barrier = pltpu.get_barrier_semaphore()
    for k in range(1, count):
        signal(barrier, row=lax.rem(me + k, count))
    signal(barrier, rep=ahead)
    signal(barrier, rep=behind)
    pl.semaphore_wait(barrier, count + 1)

    def move(dz, dc):
        to = 2 * up(dz) + lax.rem(c + dc, 2)
        k = 2 * dz + dc
        return pltpu.make_async_remote_copy(
            columns_for(to), fcat.at[rows_of(me + 1), mid],
            move_tx.at[k], move_rx.at[k], device_id={"row": to}, device_id_type=MESH,
        )

    def moved(dz, dc):
        src = 2 * down(dz) + lax.rem(c + dc, 2)
        k = 2 * dz + dc
        return src, pltpu.make_async_remote_copy(
            columns_for(src), fcat.at[rows_of(src + 1), mid],
            move_tx.at[k], move_rx.at[k], device_id={"row": src}, device_id_type=MESH,
        )

    def give_weights():
        return pltpu.make_async_remote_copy(
            w_ref, peer_w, weight_sems.at[0], weight_sems.at[1],
            device_id={"rep": ahead}, device_id_type=MESH,
        )

    def give_features(j):
        at = rows_of(j + 1)
        return pltpu.make_async_remote_copy(
            fcat.at[at, mid], peer_f.at[at, mid], feat_txs.at[j], feat_rxs.at[j],
            device_id={"rep": ahead}, device_id_type=MESH,
        )

    order = [(dz, dc) for dz in FAR_FIRST for dc in (0, 1)] + [(0, 1)]
    for dz, dc in order:
        move(dz, dc).start()
    if early:
        give_weights().start()

    @pl.loop(0, 2)
    def _(k):
        fcat[rows_of(k * (count + 1)), :] = jnp.zeros((rows, 3 * share), fcat.dtype)
        if early:
            peer_f[rows_of(k * (count + 1)), :] = jnp.zeros((rows, 3 * share), fcat.dtype)

    @pl.loop(0, count + 2)
    def _(j):
        acc[j] = jnp.zeros(acc.shape[1:], f32)

    gap = jnp.zeros((rows // cols, R, share), fcat.dtype)
    def shift(ref, at):
        x = ref[at, mid].reshape(rows // cols, cols, share)
        left = jnp.concatenate([gap, x[:, : cols - R]], axis=1)
        right = jnp.concatenate([x[:, R:], gap], axis=1)
        ref[at, pl.ds(0, share)] = left.reshape(rows, share)
        ref[at, pl.ds(2 * share, share)] = right.reshape(rows, share)

    for one in loads:
        one.wait()

    @pl.loop(0, count)
    def _(k):
        h, dc = lax.div(k, 2), lax.rem(k, 2)
        j, copy = moved(lax.rem(2 * h + lax.div(h, 2), chips), dc)
        pl.when(k > 0)(copy.wait_recv)
        if early:
            give_features(j).start()
        at = rows_of(j + 1)
        shift(fcat, at)

        @pl.loop(0, 3)
        def _(p):
            acc[j + 2 - p] += jnp.dot(
                fcat[at, :], wv[pl.ds(pl.multiple_of(p * 3 * share, share), 3 * share), :],
                preferred_element_type=f32,
            )

    def lanes(g):
        return pl.ds(pl.multiple_of(g * wide, wide), wide)

    half, inner = lax.div(z, 2), lax.rem(z, 2)
    chip_of = (z, 2 * half + 1 - inner, 2 - 2 * half + inner, 3 - 2 * half - inner)

    def pair(g, k):
        return pltpu.make_async_remote_copy(
            acc.at[2 * chip_of[k] + other + 1, :, lanes(g)], pair_rx.at[g, k],
            pair_txs.at[g, k], pair_rxs.at[g, k],
            device_id={"row": mate}, device_id_type=MESH,
        )

    def give(g, k):
        return pltpu.make_async_remote_copy(
            sum_tx.at[g, k - 1], sum_rx.at[g, k - 1], sum_txs.at[g, k], sum_rxs.at[g, k],
            device_id={"row": 2 * chip_of[2 if k == 2 else 1] + c}, device_id_type=MESH,
        )

    def block(k, core):
        return rows_of(2 * chip_of[k] + core)

    def spread(g, k):
        at = slopes.at[g, block(2 if k == 3 else 0, c)]
        return pltpu.make_async_remote_copy(
            at, at, ring_txs.at[g, k], ring_rxs.at[g, k],
            device_id={"row": 2 * chip_of[2 if k == 2 else 1] + c}, device_id_type=MESH,
        )

    def arrived(g, k):
        at = slopes.at[g, block(k, c)]
        return pltpu.make_async_remote_copy(
            at, at, ring_txs.at[g, k], ring_rxs.at[g, k],
            device_id={"row": 2 * chip_of[2 if k == 2 else 1] + c}, device_id_type=MESH,
        )

    def hand(g, k, core):
        at = slopes.at[g, block(k, core)]
        return pltpu.make_async_remote_copy(
            at, at, fwd_txs.at[g, k], fwd_rxs.at[g, k],
            device_id={"row": mate}, device_id_type=MESH,
        )

    def send_slope(g, dz):
        at = block(dz, c)
        return pltpu.make_async_remote_copy(
            slopes.at[g, at], peer_s.at[g, at], slope_txs.at[g, dz], slope_rxs.at[g, dz],
            device_id={"rep": ahead}, device_id_type=MESH,
        )

    def share_slope(g, dz, core):
        at = peer_s.at[g, block(dz, core)]
        return pltpu.make_async_remote_copy(
            at, at, share_txs.at[g, dz], share_rxs.at[g, dz],
            device_id={"row": mate}, device_id_type=MESH,
        )

    def gossip(g, p):
        return pltpu.make_async_remote_copy(
            peer_tx.at[g, p], peer_rx.at[g, p], peer_txs.at[g, p], peer_rxs.at[g, p],
            device_id={"rep": ahead}, device_id_type=MESH,
        )

    def mine(g, k):
        pair(g, k).wait_recv()
        return acc[2 * chip_of[k] + c + 1, :, lanes(g)] + pair_rx[g, k]

    def sum_near(g):
        for k in (3, 1):
            sum_tx[g, k - 1] = mine(g, k).astype(sum_tx.dtype)
            give(g, k).start()

    def sum_cross(g):
        total = mine(g, 2)
        give(g, 3).wait_recv()
        sum_tx[g, 1] = (total + sum_rx[g, 2].astype(f32)).astype(sum_tx.dtype)
        give(g, 2).start()

    def make_slope(g):
        pre = mine(g, 0)
        for k in (1, 2):
            give(g, k).wait_recv()
            pre = pre + sum_rx[g, k - 1].astype(f32)
        pre = pre * scale_in
        slope = uv[:, lanes(g)].astype(f32) * silu_slope(pre)
        slopes[g, rows_of(me), :] = slope.astype(slopes.dtype)
        for k in (2, 1):
            spread(g, k).start()
        hand(g, 0, c).start()
        if early:
            send_slope(g, 0).start()

    def gather(g):
        for k in (2, 1, 3):
            arrived(g, k).wait_recv()
            if k == 2:
                spread(g, 3).start()
            hand(g, k, c).start()
            if early:
                send_slope(g, k).start()
        for k in range(chips):
            hand(g, k, other).wait_recv()

    rate = rate_ref[0]
    height = count * rows

    def at_tap(p, q):
        at = pl.ds(pl.multiple_of(q * share, share), share)
        tap = pl.ds(pl.multiple_of((3 * p + q) * share, share), share)
        return at, tap, pl.ds(pl.multiple_of(p * rows, rows), height)

    def make_step(g):
        turned[...] = slopes[g].T

        @pl.loop(0, 3)
        def _(p):
            @pl.loop(0, 3)
            def _(q):
                at, tap, window = at_tap(p, q)
                grad = jnp.dot(turned[...], fcat[window, at], preferred_element_type=f32)
                new = wv[tap, lanes(g)].astype(f32) - rate * grad.T
                stepped[g, p, at] = new
                if not early:
                    peer_tx[g, p, at] = new.astype(peer_tx.dtype)

            if not early and not (hold and g < last):
                gossip(g, p).start()

    def shift_peer():
        give_weights().wait_recv()

        @pl.loop(0, count)
        def _(j):
            give_features(j).wait_recv()
            shift(peer_f, rows_of(j + 1))

    def gather_peer(g):
        for dz in (0,) + FAR_FIRST:
            send_slope(g, dz).wait_recv()
            share_slope(g, dz, c).start()
        for dz in (0,) + FAR_FIRST:
            share_slope(g, dz, other).wait_recv()

    def finish_early(g):
        gather_peer(g)
        peer_turned[...] = peer_s[g].T

        @pl.loop(0, 3)
        def _(p):
            @pl.loop(0, 3)
            def _(q):
                at, tap, window = at_tap(p, q)
                grad = jnp.dot(peer_turned[...], peer_f[window, at], preferred_element_type=f32)
                new = peer_w[tap, lanes(g)].astype(f32) - rate * grad.T
                mean = (stepped[g, p, at] + new) * 0.5
                out_ref[tap, lanes(g)] = mean.astype(out_ref.dtype)

    def finish(g):
        @pl.loop(0, 3)
        def _(p):
            gossip(g, p).wait_recv()

            @pl.loop(0, 3)
            def _(q):
                at, tap, _ = at_tap(p, q)
                mean = (stepped[g, p, at] + peer_rx[g, p, at].astype(f32)) * 0.5
                out_ref[tap, lanes(g)] = mean.astype(out_ref.dtype)

    for g in range(GROUPS):
        for k in (3, 1, 2, 0):
            pair(g, k).start()
    last = GROUPS - 1
    sum_near(0)
    sum_cross(0)
    sum_near(1)
    make_slope(0)
    sum_cross(1)
    gather(0)
    make_slope(1)
    make_step(0)
    gather(1)
    if early:
        make_step(1)
        shift_peer()
        for g in range(GROUPS):
            finish_early(g)
    else:
        if hold:
            for p in range(3):
                gossip(0, p).start()
        make_step(1)
        for g in range(GROUPS):
            finish(g)

    for dz, dc in order:
        move(dz, dc).wait_send()

    @pl.loop(0, GROUPS)
    def _(g):
        for dz in range(chips):
            pair(g, dz).wait_send()
            hand(g, dz, c).wait_send()
        for k in range(1, chips):
            give(g, k).wait_send()
            spread(g, k).wait_send()
        if early:
            for dz in range(chips):
                send_slope(g, dz).wait_send()
                share_slope(g, dz, c).wait_send()
        else:
            for p in range(3):
                gossip(g, p).wait_send()

    if early:
        give_weights().wait_send()

        @pl.loop(0, count)
        def _(j):
            give_features(j).wait_send()


def run_step(hop, f, w, u, rate, cols, scale_in):
    rows, chans = f.shape
    taps, outs = w.shape
    count = chans // (taps // 9)
    chips = count // 2
    share = taps // 9
    wide = outs // GROUPS
    bf, f32 = jnp.bfloat16, jnp.float32
    dma = pltpu.SemaphoreType.DMA
    anywhere = pl.BlockSpec(memory_space=pl.ANY)
    early = hop > 0
    if early:
        extra = [
            pltpu.VMEM(((count + 2) * rows, 3 * share), bf),
            pltpu.VMEM((taps, outs), bf),
            pltpu.VMEM((GROUPS, count * rows, wide), bf),
            pltpu.VMEM((wide, count * rows), bf),
            dma((2,)),
            dma((count,)), dma((count,)),
            dma((GROUPS, chips)), dma((GROUPS, chips)),
            dma((GROUPS, chips)), dma((GROUPS, chips)),
        ]
    else:
        extra = [
            pltpu.VMEM((GROUPS, 3, 3 * share, wide), bf),
            pltpu.VMEM((GROUPS, 3, 3 * share, wide), bf),
            dma((GROUPS, 3)), dma((GROUPS, 3)),
        ]
    return pl.pallas_call(
        partial(step_kernel, 1 << hop, early, hop == 0, cols, scale_in),
        out_shape=jax.ShapeDtypeStruct((taps, outs), bf),
        in_specs=[anywhere, anywhere, anywhere, pl.BlockSpec(memory_space=pltpu.SMEM)],
        out_specs=pl.BlockSpec(memory_space=pltpu.VMEM),
        scratch_shapes=[
            pltpu.VMEM(((count + 2) * rows, 3 * share), bf),
            pltpu.VMEM((taps, outs), bf),
            pltpu.VMEM((rows, outs), bf),
            pltpu.VMEM((count + 2, rows, outs), f32),
            pltpu.VMEM((GROUPS, chips, rows, wide), f32),
            pltpu.VMEM((GROUPS, chips - 1, rows, wide), bf),
            pltpu.VMEM((GROUPS, chips - 1, rows, wide), bf),
            pltpu.VMEM((GROUPS, count * rows, wide), bf),
            pltpu.VMEM((wide, count * rows), bf),
            pltpu.VMEM((GROUPS, 3, 3 * share, wide), f32),
            dma((3,)),
            dma((count,)), dma((count,)),
            dma((GROUPS, chips)), dma((GROUPS, chips)),
            dma((GROUPS, chips)), dma((GROUPS, chips)),
            dma((GROUPS, chips)), dma((GROUPS, chips)),
            dma((GROUPS, chips)), dma((GROUPS, chips)),
        ] + extra,
        compiler_params=pltpu.CompilerParams(
            collective_id=hop, has_side_effects=True, vmem_limit_bytes=48 << 20
        ),
    )(f, w, u, rate)


def per_device(features, weights, upstream, step_index):
    _, batch, rows_dev, cols, chans_in = features.shape
    share, chans_out = weights.shape[3:]
    rows_all = rows_dev * lax.axis_size("row")
    scale_in = 1.0 / (9 * chans_in) ** 0.5
    scale_grad = 1.0 / jnp.sqrt(jnp.float32(batch * rows_all * cols))
    rate = scale_grad / jnp.sqrt(1.0 + step_index.astype(jnp.float32) / 1024.0)
    f = features.reshape(rows_dev * cols, chans_in)
    w = weights.reshape(9 * share, chans_out)
    u = upstream.reshape(rows_dev * cols, chans_out)
    branches = [partial(run_step, hop, cols=cols, scale_in=scale_in) for hop in range(HOPS)]
    out = lax.switch(step_index[0] % HOPS, branches, f, w, u, rate)
    return out.reshape(weights.shape)


def solution(mesh):
    in_specs = (
        P("rep", None, "row", None, None),
        P("rep", None, None, "row", None),
        P("rep", None, "row", None, None),
        P(),
    )
    out_specs = P("rep", None, None, "row", None)
    return jax.shard_map(
        per_device, mesh=mesh, in_specs=in_specs, out_specs=out_specs, check_vma=False
    )
```

```python
from functools import partial

import jax
import jax.numpy as jnp
from jax import lax
from jax.experimental import pallas as pl
from jax.experimental.pallas import tpu as pltpu
from jax.sharding import PartitionSpec as P

R = 6
HOPS = 4
MESH = pl.DeviceIdType.MESH
FAR_FIRST = (2, 1, 3)
GROUPS = 2


def silu_slope(value):
    sig = jax.nn.sigmoid(value)
    return sig * (1.0 + value * (1.0 - sig))


def step_kernel(
    off, early, hold, cols, scale_in,
    f_ref, w_ref, u_ref, rate_ref, out_ref,
    fcat, wv, uv, acc, pair_rx, sum_tx, sum_rx, slopes, turned, stepped,
    load_sem, move_tx, move_rx, pair_txs, pair_rxs, sum_txs, sum_rxs,
    ring_txs, ring_rxs, fwd_txs, fwd_rxs, *extra,
):
    if early:
        (peer_f, peer_w, peer_s, peer_turned, weight_sems, feat_txs, feat_rxs,
         slope_txs, slope_rxs, share_txs, share_rxs) = extra
    else:
        peer_tx, peer_rx, peer_txs, peer_rxs = extra
    rows, share = uv.shape[0], fcat.shape[1] // 3
    wide = uv.shape[1] // GROUPS
    count = lax.axis_size("row")
    chips = count // 2
    reps = lax.axis_size("rep")
    me = lax.axis_index("row")
    rep = lax.axis_index("rep")
    z, c = lax.div(me, 2), lax.rem(me, 2)
    other = 1 - c
    mate = 2 * z + other
    ahead = lax.rem(rep + off, reps)
    behind = lax.rem(rep + reps - off, reps)
    f32 = jnp.float32

    def up(d):
        return lax.rem(z + d, chips)

    def down(d):
        return lax.rem(z + chips - d, chips)

    def rows_of(j):
        return pl.ds(pl.multiple_of(j * rows, rows), rows)

    def signal(sem, **to):
        pl.semaphore_signal(sem, inc=1, device_id=to, device_id_type=MESH)

    mid = pl.ds(share, share)

    def load(k, src, dst):
        return pltpu.make_async_copy(src, dst, load_sem.at[k])

    def columns_for(t):
        return f_ref.at[:, pl.ds(pl.multiple_of(t * share, share), share)]

    loads = [
        load(0, columns_for(me), fcat.at[rows_of(me + 1), mid]),
        load(1, w_ref, wv),
        load(2, u_ref, uv),
    ]
    for one in loads:
        one.start()

    barrier = pltpu.get_barrier_semaphore()
    for k in range(1, count):
        signal(barrier, row=lax.rem(me + k, count))
    signal(barrier, rep=ahead)
    signal(barrier, rep=behind)
    pl.semaphore_wait(barrier, count + 1)

    def move(dz, dc):
        to = 2 * up(dz) + lax.rem(c + dc, 2)
        k = 2 * dz + dc
        return pltpu.make_async_remote_copy(
            columns_for(to), fcat.at[rows_of(me + 1), mid],
            move_tx.at[k], move_rx.at[k], device_id={"row": to}, device_id_type=MESH,
        )

    def moved(dz, dc):
        src = 2 * down(dz) + lax.rem(c + dc, 2)
        k = 2 * dz + dc
        return src, pltpu.make_async_remote_copy(
            columns_for(src), fcat.at[rows_of(src + 1), mid],
            move_tx.at[k], move_rx.at[k], device_id={"row": src}, device_id_type=MESH,
        )

    def give_weights():
        return pltpu.make_async_remote_copy(
            w_ref, peer_w, weight_sems.at[0], weight_sems.at[1],
            device_id={"rep": ahead}, device_id_type=MESH,
        )

    def give_features(j):
        at = rows_of(j + 1)
        return pltpu.make_async_remote_copy(
            fcat.at[at, mid], peer_f.at[at, mid], feat_txs.at[j], feat_rxs.at[j],
            device_id={"rep": ahead}, device_id_type=MESH,
        )

    order = [(dz, dc) for dz in FAR_FIRST for dc in (0, 1)] + [(0, 1)]
    for dz, dc in order:
        move(dz, dc).start()
    if early:
        give_weights().start()

    @pl.loop(0, 2)
    def _(k):
        fcat[rows_of(k * (count + 1)), :] = jnp.zeros((rows, 3 * share), fcat.dtype)
        if early:
            peer_f[rows_of(k * (count + 1)), :] = jnp.zeros((rows, 3 * share), fcat.dtype)

    @pl.loop(0, count + 2)
    def _(j):
        acc[j] = jnp.zeros(acc.shape[1:], f32)

    gap = jnp.zeros((rows // cols, R, share), fcat.dtype)
    def shift(ref, at):
        x = ref[at, mid].reshape(rows // cols, cols, share)
        left = jnp.concatenate([gap, x[:, : cols - R]], axis=1)
        right = jnp.concatenate([x[:, R:], gap], axis=1)
        ref[at, pl.ds(0, share)] = left.reshape(rows, share)
        ref[at, pl.ds(2 * share, share)] = right.reshape(rows, share)

    for one in loads:
        one.wait()

    @pl.loop(0, count)
    def _(k):
        h, dc = lax.div(k, 2), lax.rem(k, 2)
        j, copy = moved(lax.rem(2 * h + lax.div(h, 2), chips), dc)
        pl.when(k > 0)(copy.wait_recv)
        if early:
            give_features(j).start()
        at = rows_of(j + 1)
        shift(fcat, at)

        @pl.loop(0, 3)
        def _(p):
            acc[j + 2 - p] += jnp.dot(
                fcat[at, :], wv[pl.ds(pl.multiple_of(p * 3 * share, share), 3 * share), :],
                preferred_element_type=f32,
            )

    def lanes(g):
        return pl.ds(pl.multiple_of(g * wide, wide), wide)

    half, inner = lax.div(z, 2), lax.rem(z, 2)
    chip_of = (z, 2 * half + 1 - inner, 2 - 2 * half + inner, 3 - 2 * half - inner)

    def pair(g, k):
        return pltpu.make_async_remote_copy(
            acc.at[2 * chip_of[k] + other + 1, :, lanes(g)], pair_rx.at[g, k],
            pair_txs.at[g, k], pair_rxs.at[g, k],
            device_id={"row": mate}, device_id_type=MESH,
        )

    def give(g, k):
        return pltpu.make_async_remote_copy(
            sum_tx.at[g, k - 1], sum_rx.at[g, k - 1], sum_txs.at[g, k], sum_rxs.at[g, k],
            device_id={"row": 2 * chip_of[2 if k == 2 else 1] + c}, device_id_type=MESH,
        )

    def block(k, core):
        return rows_of(2 * chip_of[k] + core)

    def spread(g, k):
        at = slopes.at[g, block(2 if k == 3 else 0, c)]
        return pltpu.make_async_remote_copy(
            at, at, ring_txs.at[g, k], ring_rxs.at[g, k],
            device_id={"row": 2 * chip_of[2 if k == 2 else 1] + c}, device_id_type=MESH,
        )

    def arrived(g, k):
        at = slopes.at[g, block(k, c)]
        return pltpu.make_async_remote_copy(
            at, at, ring_txs.at[g, k], ring_rxs.at[g, k],
            device_id={"row": 2 * chip_of[2 if k == 2 else 1] + c}, device_id_type=MESH,
        )

    def hand(g, k, core):
        at = slopes.at[g, block(k, core)]
        return pltpu.make_async_remote_copy(
            at, at, fwd_txs.at[g, k], fwd_rxs.at[g, k],
            device_id={"row": mate}, device_id_type=MESH,
        )

    def send_slope(g, dz):
        at = block(dz, c)
        return pltpu.make_async_remote_copy(
            slopes.at[g, at], peer_s.at[g, at], slope_txs.at[g, dz], slope_rxs.at[g, dz],
            device_id={"rep": ahead}, device_id_type=MESH,
        )

    def share_slope(g, dz, core):
        at = peer_s.at[g, block(dz, core)]
        return pltpu.make_async_remote_copy(
            at, at, share_txs.at[g, dz], share_rxs.at[g, dz],
            device_id={"row": mate}, device_id_type=MESH,
        )

    def gossip(g, p):
        return pltpu.make_async_remote_copy(
            peer_tx.at[g, p], peer_rx.at[g, p], peer_txs.at[g, p], peer_rxs.at[g, p],
            device_id={"rep": ahead}, device_id_type=MESH,
        )

    def mine(g, k):
        pair(g, k).wait_recv()
        return acc[2 * chip_of[k] + c + 1, :, lanes(g)] + pair_rx[g, k]

    def sum_near(g):
        for k in (3, 1):
            sum_tx[g, k - 1] = mine(g, k).astype(sum_tx.dtype)
            give(g, k).start()

    def sum_cross(g):
        total = mine(g, 2)
        give(g, 3).wait_recv()
        sum_tx[g, 1] = (total + sum_rx[g, 2].astype(f32)).astype(sum_tx.dtype)
        give(g, 2).start()

    def make_slope(g):
        pre = mine(g, 0)
        for k in (1, 2):
            give(g, k).wait_recv()
            pre = pre + sum_rx[g, k - 1].astype(f32)
        pre = pre * scale_in
        slope = uv[:, lanes(g)].astype(f32) * silu_slope(pre)
        slopes[g, rows_of(me), :] = slope.astype(slopes.dtype)
        for k in (2, 1):
            spread(g, k).start()
        if early:
            send_slope(g, 0).start()
        hand(g, 0, c).start()

    def gather(g):
        for k in (2, 1, 3):
            arrived(g, k).wait_recv()
            if k == 2:
                spread(g, 3).start()
            if early:
                send_slope(g, k).start()
            hand(g, k, c).start()
        for k in range(chips):
            hand(g, k, other).wait_recv()

    rate = rate_ref[0]
    height = count * rows

    def at_tap(p, q):
        at = pl.ds(pl.multiple_of(q * share, share), share)
        tap = pl.ds(pl.multiple_of((3 * p + q) * share, share), share)
        return at, tap, pl.ds(pl.multiple_of(p * rows, rows), height)

    def make_step(g):
        turned[...] = slopes[g].T

        @pl.loop(0, 3)
        def _(p):
            @pl.loop(0, 3)
            def _(q):
                at, tap, window = at_tap(p, q)
                grad = jnp.dot(turned[...], fcat[window, at], preferred_element_type=f32)
                new = wv[tap, lanes(g)].astype(f32) - rate * grad.T
                stepped[g, p, at] = new
                if not early:
                    peer_tx[g, p, at] = new.astype(peer_tx.dtype)

            if not early and not (hold and g < last):
                gossip(g, p).start()

    def shift_peer():
        give_weights().wait_recv()

        @pl.loop(0, count)
        def _(j):
            give_features(j).wait_recv()
            shift(peer_f, rows_of(j + 1))

    def gather_peer(g):
        for dz in (0,) + FAR_FIRST:
            send_slope(g, dz).wait_recv()
            share_slope(g, dz, c).start()
        for dz in (0,) + FAR_FIRST:
            share_slope(g, dz, other).wait_recv()

    def finish_early(g):
        gather_peer(g)
        peer_turned[...] = peer_s[g].T

        @pl.loop(0, 3)
        def _(p):
            @pl.loop(0, 3)
            def _(q):
                at, tap, window = at_tap(p, q)
                grad = jnp.dot(peer_turned[...], peer_f[window, at], preferred_element_type=f32)
                new = peer_w[tap, lanes(g)].astype(f32) - rate * grad.T
                mean = (stepped[g, p, at] + new) * 0.5
                out_ref[tap, lanes(g)] = mean.astype(out_ref.dtype)

    def finish(g):
        @pl.loop(0, 3)
        def _(p):
            gossip(g, p).wait_recv()

            @pl.loop(0, 3)
            def _(q):
                at, tap, _ = at_tap(p, q)
                mean = (stepped[g, p, at] + peer_rx[g, p, at].astype(f32)) * 0.5
                out_ref[tap, lanes(g)] = mean.astype(out_ref.dtype)

    for g in range(GROUPS):
        for k in (3, 1, 2, 0):
            pair(g, k).start()
    last = GROUPS - 1
    sum_near(0)
    sum_cross(0)
    sum_near(1)
    make_slope(0)
    sum_cross(1)
    gather(0)
    make_slope(1)
    make_step(0)
    gather(1)
    if early:
        make_step(1)
        shift_peer()
        for g in range(GROUPS):
            finish_early(g)
    else:
        if hold:
            for p in range(3):
                gossip(0, p).start()
        make_step(1)
        for g in range(GROUPS):
            finish(g)

    for dz, dc in order:
        move(dz, dc).wait_send()

    @pl.loop(0, GROUPS)
    def _(g):
        for dz in range(chips):
            pair(g, dz).wait_send()
            hand(g, dz, c).wait_send()
        for k in range(1, chips):
            give(g, k).wait_send()
            spread(g, k).wait_send()
        if early:
            for dz in range(chips):
                send_slope(g, dz).wait_send()
                share_slope(g, dz, c).wait_send()
        else:
            for p in range(3):
                gossip(g, p).wait_send()

    if early:
        give_weights().wait_send()

        @pl.loop(0, count)
        def _(j):
            give_features(j).wait_send()


def run_step(hop, f, w, u, rate, cols, scale_in):
    rows, chans = f.shape
    taps, outs = w.shape
    count = chans // (taps // 9)
    chips = count // 2
    share = taps // 9
    wide = outs // GROUPS
    bf, f32 = jnp.bfloat16, jnp.float32
    dma = pltpu.SemaphoreType.DMA
    anywhere = pl.BlockSpec(memory_space=pl.ANY)
    early = hop > 0
    if early:
        extra = [
            pltpu.VMEM(((count + 2) * rows, 3 * share), bf),
            pltpu.VMEM((taps, outs), bf),
            pltpu.VMEM((GROUPS, count * rows, wide), bf),
            pltpu.VMEM((wide, count * rows), bf),
            dma((2,)),
            dma((count,)), dma((count,)),
            dma((GROUPS, chips)), dma((GROUPS, chips)),
            dma((GROUPS, chips)), dma((GROUPS, chips)),
        ]
    else:
        extra = [
            pltpu.VMEM((GROUPS, 3, 3 * share, wide), bf),
            pltpu.VMEM((GROUPS, 3, 3 * share, wide), bf),
            dma((GROUPS, 3)), dma((GROUPS, 3)),
        ]
    return pl.pallas_call(
        partial(step_kernel, 1 << hop, early, hop == 0, cols, scale_in),
        out_shape=jax.ShapeDtypeStruct((taps, outs), bf),
        in_specs=[anywhere, anywhere, anywhere, pl.BlockSpec(memory_space=pltpu.SMEM)],
        out_specs=pl.BlockSpec(memory_space=pltpu.VMEM),
        scratch_shapes=[
            pltpu.VMEM(((count + 2) * rows, 3 * share), bf),
            pltpu.VMEM((taps, outs), bf),
            pltpu.VMEM((rows, outs), bf),
            pltpu.VMEM((count + 2, rows, outs), f32),
            pltpu.VMEM((GROUPS, chips, rows, wide), f32),
            pltpu.VMEM((GROUPS, chips - 1, rows, wide), bf),
            pltpu.VMEM((GROUPS, chips - 1, rows, wide), bf),
            pltpu.VMEM((GROUPS, count * rows, wide), bf),
            pltpu.VMEM((wide, count * rows), bf),
            pltpu.VMEM((GROUPS, 3, 3 * share, wide), f32),
            dma((3,)),
            dma((count,)), dma((count,)),
            dma((GROUPS, chips)), dma((GROUPS, chips)),
            dma((GROUPS, chips)), dma((GROUPS, chips)),
            dma((GROUPS, chips)), dma((GROUPS, chips)),
            dma((GROUPS, chips)), dma((GROUPS, chips)),
        ] + extra,
        compiler_params=pltpu.CompilerParams(
            collective_id=hop, has_side_effects=True, vmem_limit_bytes=48 << 20
        ),
    )(f, w, u, rate)


def per_device(features, weights, upstream, step_index):
    _, batch, rows_dev, cols, chans_in = features.shape
    share, chans_out = weights.shape[3:]
    rows_all = rows_dev * lax.axis_size("row")
    scale_in = 1.0 / (9 * chans_in) ** 0.5
    scale_grad = 1.0 / jnp.sqrt(jnp.float32(batch * rows_all * cols))
    rate = scale_grad / jnp.sqrt(1.0 + step_index.astype(jnp.float32) / 1024.0)
    f = features.reshape(rows_dev * cols, chans_in)
    w = weights.reshape(9 * share, chans_out)
    u = upstream.reshape(rows_dev * cols, chans_out)
    branches = [partial(run_step, hop, cols=cols, scale_in=scale_in) for hop in range(HOPS)]
    out = lax.switch(step_index[0] % HOPS, branches, f, w, u, rate)
    return out.reshape(weights.shape)


def solution(mesh):
    in_specs = (
        P("rep", None, "row", None, None),
        P("rep", None, None, "row", None),
        P("rep", None, "row", None, None),
        P(),
    )
    out_specs = P("rep", None, None, "row", None)
    return jax.shard_map(
        per_device, mesh=mesh, in_specs=in_specs, out_specs=out_specs, check_vma=False
    )
```
